32 devices in a mesh: grp: 2 (over y), row: 4 (over z), col: 4 (over x, core).
Axes of the slice: x: 2, y: 2, z: 4, core: 2. Of those that a mesh axis runs over, the one named last changes fastest.
Arguments:
- row_factors: float32 [12288, 128], P(('grp', 'row', 'col')), parts along dimension 0, may hold values from -1.8 to 1.8
- row_accum: float32 [12288, 128], P(('grp', 'row', 'col')), parts along dimension 0, may hold values from 10 to 2000
- row_bias: float32 [12288], P(('grp', 'row', 'col')), parts along dimension 0, may hold values from -6 to 6
- row_bias_accum: float32 [12288], P(('grp', 'row', 'col')), parts along dimension 0, may hold values from 100 to 10000
- col_factors: float32 [12288, 128], P(('grp', 'row', 'col')), parts along dimension 0, may hold values from -1.8 to 1.8
- col_accum: float32 [12288, 128], P(('grp', 'row', 'col')), parts along dimension 0, may hold values from 10 to 2000
- col_bias: float32 [12288], P(('grp', 'row', 'col')), parts along dimension 0, may hold values from -6 to 6
- col_bias_accum: float32 [12288], P(('grp', 'row', 'col')), parts along dimension 0, may hold values from 100 to 10000
- buckets: int32 [6, 12288, 384], P(None, ('grp', 'row', 'col')), parts along dimension 1, may hold values from 0 to 63
- live_pairs: int32 [6, 32], P(None, ('grp', 'row', 'col')), parts along dimension 1, may hold values 0 or 1
Outputs:
- new_row_factors: float32 [12288, 128], P(('grp', 'row', 'col')), parts along dimension 0
- new_row_bias: float32 [12288], P(('grp', 'row', 'col')), parts along dimension 0
- new_col_factors: float32 [12288, 128], P(('grp', 'row', 'col')), parts along dimension 0
- new_col_bias: float32 [12288], P(('grp', 'row', 'col')), parts along dimension 0
The draws below stay inside these ranges and needn't reach their ends.
There are 2 independent parts, one for each index of `grp`. The reference program is written for one: setup_inputs(seed, part) draws one part's arguments, and reference() takes and returns one part's arrays. A program takes and returns all parts, laid end to end along the dimension named above; each array names one. Nothing has to cross between parts.
All inputs are finite; a program needn't handle non-finite values. No bound on the sum of `live_pairs` on one device may be relied on, other than what follows from the above.
Results may differ from the reference program's by a relative error of at most 0.0003.
Values sent between devices are 32-bit elements; how exact they have to be, the bound alone decides.
A program may use at most 64 MiB of HBM per device.

```python
import math
import jax
import jax.numpy as jnp
from jax import lax

RANK = 128
BLK = 384
STEPS = 6
SWEEPS = 2
ITEMS = 6144
NBLK = 16
N_ROW = 4
N_COL = 4


def place_ends(drawn, rng, smallest, top_value):
    extent = drawn.shape
    place = [jax.random.randint(jax.random.fold_in(rng, axis), (), 0, extent[axis]) for axis in range(len(extent))]
    drawn = drawn.at[tuple(place)].set(smallest)
    longest = extent.index(max(extent))
    place[longest] = (place[longest] + 1) % extent[longest]
    return drawn.at[tuple(place)].set(top_value)


def levels(rng, extent, split, least, largest):
    def one(axis_at, parts):
        heights = jax.random.uniform(jax.random.fold_in(jax.random.fold_in(rng, 6), axis_at), (parts,), jnp.float32, least / len(split), largest / len(split))
        return jnp.repeat(jnp.exp(heights), extent[axis_at] // parts).reshape((-1,) + (1,) * (len(extent) - axis_at - 1))

    level = one(*split[0])
    for cut in split[1:]:
        level = level * one(*cut)
    return level


def normal_values(stream_key, dims, spread, most, cuts=(), kind=jnp.bfloat16):
    drawn = jax.random.normal(stream_key, dims, jnp.float32) * spread
    if len(cuts) > 0:
        drawn = levels(stream_key, dims, cuts, -0.22, 0.18) * drawn
    return jnp.clip(drawn, min=-most, max=most).astype(kind)


def setup_inputs(seed: int = 0, part: int = 0) -> dict:
    arg_keys = jax.random.split(jax.random.key(seed), 11)
    part_keys = jax.random.split(jax.random.fold_in(arg_keys[10], part), 11)
    return {
        "row_factors": normal_values(part_keys[0], (ITEMS, RANK), 0.3, 1.8, ((0, 16),), jnp.float32),
        "row_accum": jnp.clip(jnp.exp(math.log(2000.0) - 5.2983174 * jax.random.uniform(part_keys[1], (ITEMS, RANK), jnp.float32) ** levels(part_keys[1], (ITEMS, RANK), ((0, 16),), -0.2, 0.2)), 10.0, 2000.0),
        "row_bias": normal_values(part_keys[2], (ITEMS,), 1.0, 6.0, ((0, 16),), jnp.float32),
        "row_bias_accum": jnp.clip(jnp.exp(math.log(10000.0) - 4.6051702 * jax.random.uniform(part_keys[3], (ITEMS,), jnp.float32) ** levels(part_keys[3], (ITEMS,), ((0, 16),), -0.2, 0.2)), 100.0, 10000.0),
        "col_factors": normal_values(part_keys[4], (ITEMS, RANK), 0.3, 1.8, ((0, 16),), jnp.float32),
        "col_accum": jnp.clip(jnp.exp(math.log(2000.0) - 5.2983174 * jax.random.uniform(part_keys[5], (ITEMS, RANK), jnp.float32) ** levels(part_keys[5], (ITEMS, RANK), ((0, 16),), -0.2, 0.2)), 10.0, 2000.0),
        "col_bias": normal_values(part_keys[6], (ITEMS,), 1.0, 6.0, ((0, 16),), jnp.float32),
        "col_bias_accum": jnp.clip(jnp.exp(math.log(10000.0) - 4.6051702 * jax.random.uniform(part_keys[7], (ITEMS,), jnp.float32) ** levels(part_keys[7], (ITEMS,), ((0, 16),), -0.2, 0.2)), 100.0, 10000.0),
        "buckets": place_ends(jax.random.randint(part_keys[8], (STEPS, ITEMS, BLK), 0, 64), jax.random.fold_in(part_keys[8], 1), 0, 63).astype(jnp.int32),
        "live_pairs": place_ends((jax.random.randint(part_keys[9], (STEPS, NBLK), 0, 4) < 3).astype(jnp.int32), jax.random.fold_in(part_keys[9], 1), 0, 1),
    }


rate = 0.2
log_step = 0.125
log_xmax = 4.605170185988092

def one_update(u, gu, br, gbr, v, gv, bc, gbc, weight, logx):
    score = lax.dot_general(u, v, (((1,), (1,)), ((), ())), precision=lax.Precision.HIGHEST, preferred_element_type=jnp.float32)
    resid = weight * (score + br[:, None] + bc[None, :] - logx)
    grad_u = jnp.dot(resid, v, precision=lax.Precision.HIGHEST, preferred_element_type=jnp.float32)
    grad_v = lax.dot_general(resid, u, (((0,), (0,)), ((), ())), precision=lax.Precision.HIGHEST, preferred_element_type=jnp.float32)
    grad_br = lax.optimization_barrier(jnp.sum(resid, axis=1))
    grad_bc = lax.optimization_barrier(jnp.sum(resid, axis=0))
    gu = gu + grad_u * grad_u
    u = u - rate * grad_u / jnp.sqrt(gu)
    gv = gv + grad_v * grad_v
    v = v - rate * grad_v / jnp.sqrt(gv)
    gbr = gbr + grad_br * grad_br
    br = br - rate * grad_br / jnp.sqrt(gbr)
    gbc = gbc + grad_bc * grad_bc
    bc = bc - rate * grad_bc / jnp.sqrt(gbc)
    return (u, gu, br, gbr, v, gv, bc, gbc)

def update_pair(items):
    u, gu, br, gbr, v, gv, bc, gbc, bucket, live = items
    logx = bucket.astype(jnp.float32) * log_step
    weight = jnp.where(bucket > 0, jnp.minimum(1.0, jnp.exp(0.75 * (logx - log_xmax))), 0.0) * live.astype(jnp.float32)
    state = (u, gu, br, gbr, v, gv, bc, gbc)
    for sweep in range(SWEEPS):
        state = one_update(*state, weight, logx)
    return state

def reference(row_factors, row_accum, row_bias, row_bias_accum, col_factors, col_accum, col_bias, col_bias_accum, buckets, live_pairs):
    rows_n = N_ROW
    cols_n = N_COL
    count = rows_n * cols_n

    def grid(arr):
        return arr.reshape((rows_n, cols_n, BLK) + arr.shape[1:])
    rows = [grid(a) for a in (row_factors, row_accum, row_bias, row_bias_accum)]
    cols = [grid(a) for a in (col_factors, col_accum, col_bias, col_bias_accum)]
    for step in range(STEPS):
        moved_rows = [jnp.roll(a, step, axis=0).reshape((count,) + a.shape[2:]) for a in rows]
        moved_cols = [jnp.roll(a, step, axis=1).reshape((count,) + a.shape[2:]) for a in cols]
        bucket = buckets[step].reshape(count, BLK, BLK)
        live = live_pairs[step].reshape(count)
        result = lax.map(update_pair, tuple(moved_rows) + tuple(moved_cols) + (bucket, live))
        rows = [jnp.roll(a.reshape((rows_n, cols_n) + a.shape[1:]), -step, axis=0) for a in result[:4]]
        cols = [jnp.roll(a.reshape((rows_n, cols_n) + a.shape[1:]), -step, axis=1) for a in result[4:]]
    return (rows[0].reshape(row_factors.shape), rows[2].reshape(row_bias.shape), cols[0].reshape(col_factors.shape), cols[2].reshape(col_bias.shape))
```

```python
import functools

import jax
import jax.numpy as jnp
from jax import lax
from jax.experimental import pallas as pl
from jax.experimental.pallas import tpu as pltpu
from jax.sharding import PartitionSpec as P

SWEEPS = 2
LANES = 128

rate = 0.2
log_step = 0.125
log_xmax = 4.605170185988092

MESH = pl.DeviceIdType.MESH


def split(x):
    high = x.astype(jnp.bfloat16)
    low = (x - high.astype(jnp.float32)).astype(jnp.bfloat16)
    return high, low


def adagrad(value, accum, grad):
    accum = accum + grad * grad
    return value - rate * (grad * lax.rsqrt(accum)), accum


def kernel(
    n_row,
    n_col,
    row_factors,
    row_accum,
    row_bias,
    row_bias_accum,
    col_factors,
    col_accum,
    col_bias,
    col_bias_accum,
    buckets,
    live,
    out_u,
    out_br,
    out_v,
    out_bc,
    u,
    gu,
    rb,
    v,
    gv,
    cb,
    col_in,
    col_out,
    bias_home,
    bucket,
    weight,
    score_rhs,
    grad_rhs,
    grad_u,
    u_send,
    u_recv,
    gu_send,
    gu_recv,
    v_send,
    v_recv,
    in_sem,
    bucket_sem,
    home_recv,
):
    strata, tiles = u.shape[0], u.shape[1]
    half = rb.shape[1] // 2
    me_row, me_col = lax.axis_index("row"), lax.axis_index("col")

    def at_row(shift):
        return {"row": lax.rem(me_row + shift % n_row, n_row)}

    def at_col(shift):
        return {"col": lax.rem(me_col + shift % n_col, n_col)}

    loads = [
        pltpu.make_async_copy(col_factors, col_in.at[0], in_sem.at[0]),
        pltpu.make_async_copy(col_accum, col_in.at[1], in_sem.at[1]),
    ]
    for load in loads:
        load.start()
    bucket_loads = [
        pltpu.make_async_copy(buckets.at[s], bucket.at[s], bucket_sem.at[s]) for s in range(strata)
    ]
    bucket_loads[0].start()
    for k in range(tiles):
        rows = pl.ds(k * LANES, LANES)
        pltpu.make_async_copy(row_factors.at[rows], u.at[0, k], u_recv.at[0, k]).start()
    for k in range(tiles):
        rows = pl.ds(k * LANES, LANES)
        pltpu.make_async_copy(row_accum.at[rows], gu.at[0, k], gu_recv.at[0, k]).start()
    for load in bucket_loads[1:]:
        load.start()

    barrier = pltpu.get_barrier_semaphore()
    partners = 0
    for at, n in ((at_row, n_row), (at_col, n_col)):
        for shift in sorted({1, n - 1, (strata - 1) % n, -(strata - 1) % n} - {0}):
            pl.semaphore_signal(barrier, inc=1, device_id=at(shift), device_id_type=MESH)
            partners += 1
    pl.semaphore_wait(barrier, partners)

    rb[0, 0:tiles, :] = row_bias[...]
    rb[0, half : half + tiles, :] = row_bias_accum[...]
    cb[0, 0:tiles, :] = col_bias[...]
    cb[0, half : half + tiles, :] = col_bias_accum[...]

    def prepare(s):
        count = bucket[s]
        logx = count.astype(jnp.float32) * log_step
        weight[...] = jnp.where(
            count > 0, jnp.minimum(1.0, jnp.exp(0.75 * (logx - log_xmax))), 0.0
        ) * live[s, 0].astype(jnp.float32)

    bucket_loads[0].wait()
    prepare(0)
    for load in loads:
        load.wait()
    v[0] = col_in[0].T
    gv[0] = col_in[1].T

    def send_u(s, k):
        return pltpu.make_async_remote_copy(
            src_ref=u.at[s, k], dst_ref=u.at[s + 1, k], send_sem=u_send.at[s, k],
            recv_sem=u_recv.at[s + 1, k], device_id=at_row(1), device_id_type=MESH)

    def send_gu(s, k):
        return pltpu.make_async_remote_copy(
            src_ref=gu.at[s, k], dst_ref=gu.at[s + 1, k], send_sem=gu_send.at[s, k],
            recv_sem=gu_recv.at[s + 1, k], device_id=at_row(1), device_id_type=MESH)

    def send_v(s, which):
        ref = (v, gv, cb, rb)[which]
        return pltpu.make_async_remote_copy(
            src_ref=ref.at[s], dst_ref=ref.at[s + 1], send_sem=v_send.at[s, which],
            recv_sem=v_recv.at[s + 1, which], device_id=at_row(1) if which == 3 else at_col(1),
            device_id_type=MESH)

    def home(src, dst, which, to):
        return pltpu.make_async_remote_copy(
            src_ref=src, dst_ref=dst, send_sem=v_send.at[strata - 1 + which // 4, which % 4],
            recv_sem=home_recv.at[which], device_id=to, device_id_type=MESH)

    last = strata - 1
    home_row, home_col = at_row(-last), at_col(-last)

    def home_u(k):
        return home(u.at[last, k], out_u.at[pl.ds(k * LANES, LANES)], k, home_row)

    def home_br():
        return home(rb.at[last], bias_home.at[0], tiles, home_row)

    def home_v():
        return home(col_out, out_v, tiles + 1, home_col)

    def home_bc():
        return home(cb.at[last], bias_home.at[1], tiles + 2, home_col)

    def lane_parts(x):
        return [x[:, j * LANES : (j + 1) * LANES] for j in range(tiles)]

    def split_cols(cols):
        high, low = split(cols)
        score_rhs[...] = jnp.concatenate([high, high, low], axis=0)
        grad_rhs[...] = jnp.concatenate([high, low], axis=0)

    def bias_row(s):
        return jnp.concatenate([cb[s, j : j + 1, :] for j in range(tiles)], axis=1)

    def tile_grads(s, k, rows, bc):
        high, low = split(rows)
        score = jnp.dot(
            jnp.concatenate([high, low, high], axis=1), score_rhs[...],
            preferred_element_type=jnp.float32)
        br = jnp.broadcast_to(rb[s, k : k + 1, :], (LANES, LANES)).T
        br = jnp.concatenate([br] * tiles, axis=1)
        span = pl.ds(k * LANES, LANES)
        logx = bucket[s, span, :].astype(jnp.float32) * log_step
        resid = weight[span, :] * (score + br + bc - logx)
        res_high, res_low = split(resid)
        four = lax.dot_general(
            jnp.concatenate([res_high, res_low], axis=0), grad_rhs[...],
            (((1,), (1,)), ((), ())), preferred_element_type=jnp.float32)
        rank = rows.shape[1]
        du = (four[:LANES, :rank] + four[:LANES, rank:]) + (four[LANES:, :rank] + four[LANES:, rank:])
        turned_high, turned_low = split(rows.T)
        dv = jnp.dot(
            jnp.concatenate([turned_high, turned_low, turned_high], axis=1),
            jnp.concatenate([res_high, res_high, res_low], axis=0),
            preferred_element_type=jnp.float32)
        parts = lane_parts(resid)
        dbr = jnp.sum(functools.reduce(jnp.add, parts).T, axis=0, keepdims=True)
        dbc = jnp.sum(resid, axis=0, keepdims=True)
        new_br, new_gbr = adagrad(rb[s, k : k + 1, :], rb[s, half + k : half + k + 1, :], dbr)
        rb[s, k : k + 1, :] = new_br
        rb[s, half + k : half + k + 1, :] = new_gbr
        return du, dv, dbc

    def update_cols(s, dv, dbc):
        v[s], gv[s] = adagrad(v[s], gv[s], dv)
        for j, part in enumerate(lane_parts(dbc)):
            new_bc, new_gbc = adagrad(cb[s, j : j + 1, :], cb[s, half + j : half + j + 1, :], part)
            cb[s, j : j + 1, :] = new_bc
            cb[s, half + j : half + j + 1, :] = new_gbc

    def arrived(ref, sem):
        pltpu.make_async_copy(ref, ref, sem).wait()

    @pl.loop(0, strata)
    def _(s):
        @pl.when(s > 0)
        def _():
            for which, ref in ((3, rb), (2, cb), (0, v)):
                arrived(ref.at[s], v_recv.at[s, which])

        split_cols(v[s])
        bc = bias_row(s)
        dv, dbc = 0.0, 0.0
        for k in range(tiles):
            arrived(u.at[s, k], u_recv.at[s, k])
            du, more_dv, more_dbc = tile_grads(s, k, u[s, k], bc)
            grad_u[k] = du
            dv, dbc = dv + more_dv, dbc + more_dbc

        @pl.when(s > 0)
        def _():
            arrived(gv.at[s], v_recv.at[s, 1])

        update_cols(s, dv, dbc)

        split_cols(v[s])
        bc = bias_row(s)
        dv, dbc = 0.0, 0.0
        for k in range(tiles):
            arrived(gu.at[s, k], gu_recv.at[s, k])
            rows, accum = adagrad(u[s, k], gu[s, k], grad_u[k])
            du, more_dv, more_dbc = tile_grads(s, k, rows, bc)
            dv, dbc = dv + more_dv, dbc + more_dbc
            u[s, k], gu[s, k] = adagrad(rows, accum, du)

            @pl.when(s < last)
            def _():
                send_u(s, k).start()

            @pl.when(s == last)
            def _():
                home_u(k).start()

        update_cols(s, dv, dbc)

        @pl.when(s < last)
        def _():
            send_v(s, 3).start()
            send_v(s, 2).start()
            send_v(s, 0).start()
            for k in range(tiles):
                send_gu(s, k).start()
            send_v(s, 1).start()
            pltpu.make_async_copy(buckets.at[s + 1], bucket.at[s + 1], bucket_sem.at[s + 1]).wait()
            prepare(s + 1)

    home_br().start()
    home_bc().start()
    col_out[...] = v[last].T
    home_v().start()

    @pl.loop(0, last)
    def _(s):
        for k in range(tiles):
            send_u(s, k).wait_send()
            send_gu(s, k).wait_send()
        for which in range(4):
            send_v(s, which).wait_send()

    home_br().wait()
    home_bc().wait()
    out_br[...] = bias_home[0, 0:tiles, :]
    out_bc[...] = bias_home[1, 0:tiles, :]
    for k in range(tiles):
        home_u(k).wait()
    home_v().wait()


def shards(
    n_row,
    n_col,
    row_factors,
    row_accum,
    row_bias,
    row_bias_accum,
    col_factors,
    col_accum,
    col_bias,
    col_bias_accum,
    buckets,
    live_pairs,
):
    strata, block, _ = buckets.shape
    rank = row_factors.shape[1]
    tiles = block // LANES
    biases = [b.reshape(tiles, LANES) for b in (row_bias, row_bias_accum, col_bias, col_bias_accum)]
    packed = 2 * (-(-tiles // 4) * 4)
    f32, bf16 = jnp.float32, jnp.bfloat16
    anywhere = pl.BlockSpec(memory_space=pl.ANY)
    vmem = pl.BlockSpec(memory_space=pltpu.VMEM)
    smem = pl.BlockSpec(memory_space=pltpu.SMEM)
    dma = pltpu.SemaphoreType.DMA
    factors = jax.ShapeDtypeStruct((block, rank), f32)
    bias = jax.ShapeDtypeStruct((tiles, LANES), f32)
    new_u, new_br, new_v, new_bc = pl.pallas_call(
        functools.partial(kernel, n_row, n_col),
        out_shape=(factors, bias, factors, bias),
        in_specs=[anywhere, anywhere, vmem, vmem, anywhere, anywhere, vmem, vmem, anywhere, smem],
        out_specs=(anywhere, vmem, anywhere, vmem),
        scratch_shapes=[
            pltpu.VMEM((strata, tiles, LANES, rank), f32),
            pltpu.VMEM((strata, tiles, LANES, rank), f32),
            pltpu.VMEM((strata, packed, LANES), f32),
            pltpu.VMEM((strata, rank, block), f32),
            pltpu.VMEM((strata, rank, block), f32),
            pltpu.VMEM((strata, packed, LANES), f32),
            pltpu.VMEM((2, block, rank), f32),
            pltpu.VMEM((block, rank), f32),
            pltpu.VMEM((2, packed, LANES), f32),
            pltpu.VMEM((strata, block, block), jnp.int32),
            pltpu.VMEM((block, block), f32),
            pltpu.VMEM((3 * rank, block), bf16),
            pltpu.VMEM((2 * rank, block), bf16),
            pltpu.VMEM((tiles, LANES, rank), f32),
            dma((strata, tiles)),
            dma((strata, tiles)),
            dma((strata, tiles)),
            dma((strata, tiles)),
            dma((strata + 2, 4)),
            dma((strata, 4)),
            dma((2,)),
            dma((strata,)),
            dma((tiles + 3,)),
        ],
        compiler_params=pltpu.CompilerParams(
            collective_id=0, has_side_effects=True, vmem_limit_bytes=40 * 1024 * 1024
        ),
    )(
        row_factors, row_accum, biases[0], biases[1],
        col_factors, col_accum, biases[2], biases[3],
        buckets, live_pairs,
    )
    return (new_u, new_br.reshape(block), new_v, new_bc.reshape(block))


def solution(mesh):
    in_specs = (
        P(("grp", "row", "col"), None),
        P(("grp", "row", "col"), None),
        P(("grp", "row", "col")),
        P(("grp", "row", "col")),
        P(("grp", "row", "col"), None),
        P(("grp", "row", "col"), None),
        P(("grp", "row", "col")),
        P(("grp", "row", "col")),
        P(None, ("grp", "row", "col"), None),
        P(None, ("grp", "row", "col")),
    )
    out_specs = (
        P(("grp", "row", "col"), None),
        P(("grp", "row", "col")),
        P(("grp", "row", "col"), None),
        P(("grp", "row", "col")),
    )
    body = functools.partial(shards, mesh.shape["row"], mesh.shape["col"])
    return jax.shard_map(body, mesh=mesh, in_specs=in_specs, out_specs=out_specs, check_vma=False)
```

```python
import functools

import jax
import jax.numpy as jnp
from jax import lax
from jax.experimental import pallas as pl
from jax.experimental.pallas import tpu as pltpu
from jax.sharding import PartitionSpec as P

SWEEPS = 2
LANES = 128
VMEM_BYTES = 63 * 1024 * 1024

rate = 0.2
log_step = 0.125
log_xmax = 4.605170185988092

MESH = pl.DeviceIdType.MESH


def split(x):
    high = x.astype(jnp.bfloat16)
    low = (x - high.astype(jnp.float32)).astype(jnp.bfloat16)
    return high, low


def adagrad(value, accum, grad):
    accum = accum + grad * grad
    return value - rate * (grad * lax.rsqrt(accum)), accum


def write_out(*refs):
    ins, outs, staged, sem = refs[:4], refs[4:8], refs[8:12], refs[12]
    loads = [pltpu.make_async_copy(ins[i], staged[i], sem.at[0, i]) for i in range(4)]
    stores = [pltpu.make_async_copy(staged[i], outs[i], sem.at[1, i]) for i in range(4)]
    for load in loads:
        load.start()
    for load, store in zip(loads, stores):
        load.wait()
        store.start()
    for store in stores:
        store.wait()


def kernel(
    n_row,
    n_col,
    row_factors,
    row_accum,
    row_bias,
    row_bias_accum,
    col_factors,
    col_accum,
    col_bias,
    col_bias_accum,
    buckets,
    live,
    out_u,
    out_br,
    out_v,
    out_bc,
    u,
    gu,
    rb,
    v,
    gv,
    cb,
    col_in,
    bias_in,
    col_out,
    bias_home,
    bucket,
    weight,
    score_rhs,
    grad_rhs,
    grad_u,
    u_send,
    u_recv,
    gu_send,
    gu_recv,
    v_send,
    v_recv,
    in_sem,
    bucket_sem,
    home_recv,
):
    strata, tiles = u.shape[0], u.shape[1]
    half = rb.shape[1] // 2
    me_row, me_col = lax.axis_index("row"), lax.axis_index("col")

    def at_row(shift):
        return {"row": lax.rem(me_row + shift % n_row, n_row)}

    def at_col(shift):
        return {"col": lax.rem(me_col + shift % n_col, n_col)}

    loads = [
        pltpu.make_async_copy(col_factors, col_in.at[0], in_sem.at[0]),
        pltpu.make_async_copy(col_accum, col_in.at[1], in_sem.at[1]),
    ]
    for load in loads:
        load.start()
    bucket_loads = [
        pltpu.make_async_copy(buckets.at[s], bucket.at[s], bucket_sem.at[s]) for s in range(strata)
    ]
    bucket_loads[0].start()
    bias_loads = [
        pltpu.make_async_copy(ref, bias_in.at[i], in_sem.at[2 + i])
        for i, ref in enumerate((row_bias, row_bias_accum, col_bias, col_bias_accum))
    ]
    for load in bias_loads:
        load.start()
    for k in range(tiles):
        rows = pl.ds(k * LANES, LANES)
        pltpu.make_async_copy(row_factors.at[rows], u.at[0, k], u_recv.at[0, k]).start()
    for k in range(tiles):
        rows = pl.ds(k * LANES, LANES)
        pltpu.make_async_copy(row_accum.at[rows], gu.at[0, k], gu_recv.at[0, k]).start()
    for load in bucket_loads[1:]:
        load.start()

    barrier = pltpu.get_barrier_semaphore()
    partners = 0
    for at, n in ((at_row, n_row), (at_col, n_col)):
        for shift in sorted({1, n - 1, (strata - 1) % n, -(strata - 1) % n} - {0}):
            pl.semaphore_signal(barrier, inc=1, device_id=at(shift), device_id_type=MESH)
            partners += 1
    pl.semaphore_wait(barrier, partners)

    for load in bias_loads:
        load.wait()
    rb[0, 0:tiles, :] = bias_in[0]
    rb[0, half : half + tiles, :] = bias_in[1]
    cb[0, 0:tiles, :] = bias_in[2]
    cb[0, half : half + tiles, :] = bias_in[3]

    def prepare(s):
        count = bucket[s]
        logx = count.astype(jnp.float32) * log_step
        weight[...] = jnp.where(
            count > 0, jnp.minimum(1.0, jnp.exp(0.75 * (logx - log_xmax))), 0.0
        ) * live[0, s].astype(jnp.float32)

    bucket_loads[0].wait()
    prepare(0)
    for load in loads:
        load.wait()
    v[0] = col_in[0].T
    gv[0] = col_in[1].T

    def send_u(s, k):
        return pltpu.make_async_remote_copy(
            src_ref=u.at[s, k], dst_ref=u.at[s + 1, k], send_sem=u_send.at[s, k],
            recv_sem=u_recv.at[s + 1, k], device_id=at_row(1), device_id_type=MESH)

    def send_gu(s, k):
        return pltpu.make_async_remote_copy(
            src_ref=gu.at[s, k], dst_ref=gu.at[s + 1, k], send_sem=gu_send.at[s, k],
            recv_sem=gu_recv.at[s + 1, k], device_id=at_row(1), device_id_type=MESH)

    def send_v(s, which):
        ref = (v, gv, cb, rb)[which]
        return pltpu.make_async_remote_copy(
            src_ref=ref.at[s], dst_ref=ref.at[s + 1], send_sem=v_send.at[s, which],
            recv_sem=v_recv.at[s + 1, which], device_id=at_row(1) if which == 3 else at_col(1),
            device_id_type=MESH)

    def home(src, dst, which, to):
        return pltpu.make_async_remote_copy(
            src_ref=src, dst_ref=dst, send_sem=v_send.at[strata - 1 + which // 4, which % 4],
            recv_sem=home_recv.at[which], device_id=to, device_id_type=MESH)

    last = strata - 1
    home_row, home_col = at_row(-last), at_col(-last)

    def home_u(k):
        return home(u.at[last, k], out_u.at[pl.ds(k * LANES, LANES)], k, home_row)

    def home_br():
        return home(rb.at[last], bias_home.at[0], tiles, home_row)

    def home_v():
        return home(col_out, out_v, tiles + 1, home_col)

    def home_bc():
        return home(cb.at[last], bias_home.at[1], tiles + 2, home_col)

    def lane_parts(x):
        return [x[:, j * LANES : (j + 1) * LANES] for j in range(tiles)]

    def split_cols(cols):
        high, low = split(cols)
        score_rhs[...] = jnp.concatenate([high, high, low], axis=0)
        grad_rhs[...] = jnp.concatenate([high, low], axis=0)

    def bias_row(s):
        return jnp.concatenate([cb[s, j : j + 1, :] for j in range(tiles)], axis=1)

    def tile_grads(s, k, rows, bc):
        high, low = split(rows)
        score = jnp.dot(
            jnp.concatenate([high, low, high], axis=1), score_rhs[...],
            preferred_element_type=jnp.float32)
        br = jnp.broadcast_to(rb[s, k : k + 1, :], (LANES, LANES)).T
        br = jnp.concatenate([br] * tiles, axis=1)
        span = pl.ds(k * LANES, LANES)
        logx = bucket[s, span, :].astype(jnp.float32) * log_step
        resid = weight[span, :] * (score + br + bc - logx)
        res_high, res_low = split(resid)
        four = lax.dot_general(
            jnp.concatenate([res_high, res_low], axis=0), grad_rhs[...],
            (((1,), (1,)), ((), ())), preferred_element_type=jnp.float32)
        rank = rows.shape[1]
        du = (four[:LANES, :rank] + four[:LANES, rank:]) + (four[LANES:, :rank] + four[LANES:, rank:])
        turned_high, turned_low = split(rows.T)
        dv = jnp.dot(
            jnp.concatenate([turned_high, turned_low, turned_high], axis=1),
            jnp.concatenate([res_high, res_high, res_low], axis=0),
            preferred_element_type=jnp.float32)
        parts = lane_parts(resid)
        dbr = jnp.sum(functools.reduce(jnp.add, parts).T, axis=0, keepdims=True)
        dbc = jnp.sum(resid, axis=0, keepdims=True)
        new_br, new_gbr = adagrad(rb[s, k : k + 1, :], rb[s, half + k : half + k + 1, :], dbr)
        rb[s, k : k + 1, :] = new_br
        rb[s, half + k : half + k + 1, :] = new_gbr
        return du, dv, dbc

    def update_cols(s, dv, dbc):
        v[s], gv[s] = adagrad(v[s], gv[s], dv)
        for j, part in enumerate(lane_parts(dbc)):
            new_bc, new_gbc = adagrad(cb[s, j : j + 1, :], cb[s, half + j : half + j + 1, :], part)
            cb[s, j : j + 1, :] = new_bc
            cb[s, half + j : half + j + 1, :] = new_gbc

    def arrived(ref, sem):
        pltpu.make_async_copy(ref, ref, sem).wait()

    @pl.loop(0, strata)
    def _(s):
        @pl.when(s > 0)
        def _():
            for which, ref in ((3, rb), (2, cb), (0, v)):
                arrived(ref.at[s], v_recv.at[s, which])

        split_cols(v[s])
        bc = bias_row(s)
        dv, dbc = 0.0, 0.0
        for k in range(tiles):
            arrived(u.at[s, k], u_recv.at[s, k])
            du, more_dv, more_dbc = tile_grads(s, k, u[s, k], bc)
            grad_u[k] = du
            dv, dbc = dv + more_dv, dbc + more_dbc

        @pl.when(s > 0)
        def _():
            arrived(gv.at[s], v_recv.at[s, 1])

        update_cols(s, dv, dbc)

        split_cols(v[s])
        bc = bias_row(s)
        dv, dbc = 0.0, 0.0
        for k in range(tiles):
            arrived(gu.at[s, k], gu_recv.at[s, k])
            rows, accum = adagrad(u[s, k], gu[s, k], grad_u[k])
            du, more_dv, more_dbc = tile_grads(s, k, rows, bc)
            dv, dbc = dv + more_dv, dbc + more_dbc
            u[s, k], gu[s, k] = adagrad(rows, accum, du)

            @pl.when(s < last)
            def _():
                send_u(s, k).start()

            @pl.when(s == last)
            def _():
                home_u(k).start()

        update_cols(s, dv, dbc)

        @pl.when(s < last)
        def _():
            send_v(s, 3).start()
            send_v(s, 2).start()
            send_v(s, 0).start()
            pltpu.make_async_copy(buckets.at[s + 1], bucket.at[s + 1], bucket_sem.at[s + 1]).wait()
            prepare(s + 1)
            send_v(s, 0).wait_send()
            send_v(s, 1).start()
            for k in range(tiles):
                send_u(s, k).wait_send()
                send_gu(s, k).start()

    home_br().start()
    home_bc().start()
    col_out[...] = v[last].T
    home_v().start()

    @pl.loop(0, last)
    def _(s):
        for k in range(tiles):
            send_gu(s, k).wait_send()
        for which in range(1, 4):
            send_v(s, which).wait_send()

    home_br().wait()
    home_bc().wait()
    out_br[...] = bias_home[0, 0:tiles, :]
    out_bc[...] = bias_home[1, 0:tiles, :]
    for k in range(tiles):
        home_u(k).wait()
    home_v().wait()


def shards(
    n_row,
    n_col,
    row_factors,
    row_accum,
    row_bias,
    row_bias_accum,
    col_factors,
    col_accum,
    col_bias,
    col_bias_accum,
    buckets,
    live_pairs,
):
    strata, block, _ = buckets.shape
    rank = row_factors.shape[1]
    tiles = block // LANES
    biases = [b.reshape(tiles, LANES) for b in (row_bias, row_bias_accum, col_bias, col_bias_accum)]
    packed = 2 * (-(-tiles // 4) * 4)
    f32, bf16 = jnp.float32, jnp.bfloat16
    hbm = pl.BlockSpec(memory_space=pltpu.HBM)
    vmem = pl.BlockSpec(memory_space=pltpu.VMEM)
    smem = pl.BlockSpec(memory_space=pltpu.SMEM)
    dma = pltpu.SemaphoreType.DMA
    factors = jax.ShapeDtypeStruct((block, rank), f32)
    bias = jax.ShapeDtypeStruct((tiles, LANES), f32)
    new_u, new_br, new_v, new_bc = pl.pallas_call(
        functools.partial(kernel, n_row, n_col),
        out_shape=(factors, bias, factors, bias),
        in_specs=[hbm] * 9 + [smem],
        out_specs=(hbm, vmem, hbm, vmem),
        scratch_shapes=[
            pltpu.VMEM((strata, tiles, LANES, rank), f32),
            pltpu.VMEM((strata, tiles, LANES, rank), f32),
            pltpu.VMEM((strata, packed, LANES), f32),
            pltpu.VMEM((strata, rank, block), f32),
            pltpu.VMEM((strata, rank, block), f32),
            pltpu.VMEM((strata, packed, LANES), f32),
            pltpu.VMEM((2, block, rank), f32),
            pltpu.VMEM((4, tiles, LANES), f32),
            pltpu.VMEM((block, rank), f32),
            pltpu.VMEM((2, packed, LANES), f32),
            pltpu.VMEM((strata, block, block), jnp.int32),
            pltpu.VMEM((block, block), f32),
            pltpu.VMEM((3 * rank, block), bf16),
            pltpu.VMEM((2 * rank, block), bf16),
            pltpu.VMEM((tiles, LANES, rank), f32),
            dma((strata, tiles)),
            dma((strata, tiles)),
            dma((strata, tiles)),
            dma((strata, tiles)),
            dma((strata + 2, 4)),
            dma((strata, 4)),
            dma((6,)),
            dma((strata,)),
            dma((tiles + 3,)),
        ],
        compiler_params=pltpu.CompilerParams(
            collective_id=0, has_side_effects=True, vmem_limit_bytes=VMEM_BYTES
        ),
    )(
        row_factors, row_accum, biases[0], biases[1],
        col_factors, col_accum, biases[2], biases[3],
        buckets, live_pairs.T,
    )
    new_u, new_br, new_v, new_bc = pl.pallas_call(
        write_out,
        out_shape=(factors, bias, factors, bias),
        in_specs=[hbm] * 4,
        out_specs=(hbm,) * 4,
        scratch_shapes=[
            pltpu.VMEM((block, rank), f32),
            pltpu.VMEM((tiles, LANES), f32),
            pltpu.VMEM((block, rank), f32),
            pltpu.VMEM((tiles, LANES), f32),
            dma((2, 4)),
        ],
        compiler_params=pltpu.CompilerParams(vmem_limit_bytes=VMEM_BYTES),
    )(new_u, new_br, new_v, new_bc)
    return (new_u, new_br.reshape(block), new_v, new_bc.reshape(block))


def solution(mesh):
    in_specs = (
        P(("grp", "row", "col"), None),
        P(("grp", "row", "col"), None),
        P(("grp", "row", "col")),
        P(("grp", "row", "col")),
        P(("grp", "row", "col"), None),
        P(("grp", "row", "col"), None),
        P(("grp", "row", "col")),
        P(("grp", "row", "col")),
        P(None, ("grp", "row", "col"), None),
        P(None, ("grp", "row", "col")),
    )
    out_specs = (
        P(("grp", "row", "col"), None),
        P(("grp", "row", "col")),
        P(("grp", "row", "col"), None),
        P(("grp", "row", "col")),
    )
    body = functools.partial(shards, mesh.shape["row"], mesh.shape["col"])
    return jax.shard_map(body, mesh=mesh, in_specs=in_specs, out_specs=out_specs, check_vma=False)
```

```python
import functools

import jax
import jax.numpy as jnp
from jax import lax
from jax.experimental import pallas as pl
from jax.experimental.pallas import tpu as pltpu
from jax.sharding import PartitionSpec as P

SWEEPS = 2
LANES = 128
VMEM_BYTES = 63 * 1024 * 1024

rate = 0.2
log_step = 0.125
log_xmax = 4.605170185988092

MESH = pl.DeviceIdType.MESH


def split(x):
    high = x.astype(jnp.bfloat16)
    low = (x - high.astype(jnp.float32)).astype(jnp.bfloat16)
    return high, low


def adagrad(value, accum, grad):
    accum = accum + grad * grad
    return value - rate * (grad * lax.rsqrt(accum)), accum


def write_out(*refs):
    ins, outs, staged, sem = refs[:4], refs[4:8], refs[8:12], refs[12]
    loads = [pltpu.make_async_copy(ins[i], staged[i], sem.at[0, i]) for i in range(4)]
    stores = [pltpu.make_async_copy(staged[i], outs[i], sem.at[1, i]) for i in range(4)]
    for load in loads:
        load.start()
    for load, store in zip(loads, stores):
        load.wait()
        store.start()
    for store in stores:
        store.wait()


def kernel(
    n_row,
    n_col,
    row_factors,
    row_accum,
    row_bias,
    row_bias_accum,
    col_factors,
    col_accum,
    col_bias,
    col_bias_accum,
    buckets,
    live,
    out_u,
    out_br,
    out_v,
    out_bc,
    u,
    gu,
    rb,
    v,
    gv,
    cb,
    col_in,
    bias_in,
    col_out,
    bias_home,
    bucket,
    weight,
    score_rhs,
    grad_rhs,
    grad_u,
    u_send,
    u_recv,
    gu_send,
    gu_recv,
    v_send,
    v_recv,
    in_sem,
    bucket_sem,
    home_recv,
):
    strata, tiles = u.shape[0], u.shape[1]
    half = rb.shape[1] // 2
    me_row, me_col = lax.axis_index("row"), lax.axis_index("col")

    def at_row(shift):
        return {"row": lax.rem(me_row + shift % n_row, n_row)}

    def at_col(shift):
        return {"col": lax.rem(me_col + shift % n_col, n_col)}

    loads = [
        pltpu.make_async_copy(col_factors, col_in.at[0], in_sem.at[0]),
        pltpu.make_async_copy(col_accum, col_in.at[1], in_sem.at[1]),
    ]
    for load in loads:
        load.start()
    bucket_loads = [
        pltpu.make_async_copy(buckets.at[s], bucket.at[s], bucket_sem.at[s]) for s in range(strata)
    ]
    bucket_loads[0].start()
    bias_loads = [
        pltpu.make_async_copy(ref, bias_in.at[i], in_sem.at[2 + i])
        for i, ref in enumerate((row_bias, row_bias_accum, col_bias, col_bias_accum))
    ]
    for load in bias_loads:
        load.start()
    for k in range(tiles):
        rows = pl.ds(k * LANES, LANES)
        pltpu.make_async_copy(row_factors.at[rows], u.at[0, k], u_recv.at[0, k]).start()
    for k in range(tiles):
        rows = pl.ds(k * LANES, LANES)
        pltpu.make_async_copy(row_accum.at[rows], gu.at[0, k], gu_recv.at[0, k]).start()
    for load in bucket_loads[1:]:
        load.start()

    barrier = pltpu.get_barrier_semaphore()
    partners = 0
    for at, n in ((at_row, n_row), (at_col, n_col)):
        for shift in sorted({1, n - 1, (strata - 1) % n, -(strata - 1) % n} - {0}):
            pl.semaphore_signal(barrier, inc=1, device_id=at(shift), device_id_type=MESH)
            partners += 1

    for load in bias_loads:
        load.wait()
    rb[0, 0:tiles, :] = bias_in[0]
    rb[0, half : half + tiles, :] = bias_in[1]
    cb[0, 0:tiles, :] = bias_in[2]
    cb[0, half : half + tiles, :] = bias_in[3]

    def prepare(s):
        count = bucket[s]
        logx = count.astype(jnp.float32) * log_step
        weight[...] = jnp.where(
            count > 0, jnp.minimum(1.0, jnp.exp(0.75 * (logx - log_xmax))), 0.0
        ) * live[0, s].astype(jnp.float32)

    bucket_loads[0].wait()
    prepare(0)
    for load in loads:
        load.wait()
    v[0] = col_in[0].T
    gv[0] = col_in[1].T

    def send_u(s, k):
        return pltpu.make_async_remote_copy(
            src_ref=u.at[s, k], dst_ref=u.at[s + 1, k], send_sem=u_send.at[s, k],
            recv_sem=u_recv.at[s + 1, k], device_id=at_row(1), device_id_type=MESH)

    def send_gu(s, k):
        return pltpu.make_async_remote_copy(
            src_ref=gu.at[s, k], dst_ref=gu.at[s + 1, k], send_sem=gu_send.at[s, k],
            recv_sem=gu_recv.at[s + 1, k], device_id=at_row(1), device_id_type=MESH)

    def send_v(s, which):
        ref = (v, gv, cb, rb)[which]
        return pltpu.make_async_remote_copy(
            src_ref=ref.at[s], dst_ref=ref.at[s + 1], send_sem=v_send.at[s, which],
            recv_sem=v_recv.at[s + 1, which], device_id=at_row(1) if which == 3 else at_col(1),
            device_id_type=MESH)

    def home(src, dst, which, to):
        return pltpu.make_async_remote_copy(
            src_ref=src, dst_ref=dst, send_sem=v_send.at[strata - 1 + which // 4, which % 4],
            recv_sem=home_recv.at[which], device_id=to, device_id_type=MESH)

    last = strata - 1
    home_row, home_col = at_row(-last), at_col(-last)

    def home_u(k):
        return home(u.at[last, k], out_u.at[pl.ds(k * LANES, LANES)], k, home_row)

    def home_br():
        return home(rb.at[last], bias_home.at[0], tiles, home_row)

    def home_v():
        return home(col_out, out_v, tiles + 1, home_col)

    def home_bc():
        return home(cb.at[last], bias_home.at[1], tiles + 2, home_col)

    def lane_parts(x):
        return [x[:, j * LANES : (j + 1) * LANES] for j in range(tiles)]

    def split_cols(cols):
        high, low = split(cols)
        score_rhs[...] = jnp.concatenate([high, high, low], axis=0)
        grad_rhs[...] = jnp.concatenate([high, low], axis=0)

    def bias_row(s):
        return jnp.concatenate([cb[s, j : j + 1, :] for j in range(tiles)], axis=1)

    def tile_grads(s, k, rows, bc):
        high, low = split(rows)
        score = jnp.dot(
            jnp.concatenate([high, low, high], axis=1), score_rhs[...],
            preferred_element_type=jnp.float32)
        br = jnp.broadcast_to(rb[s, k : k + 1, :], (LANES, LANES)).T
        br = jnp.concatenate([br] * tiles, axis=1)
        span = pl.ds(k * LANES, LANES)
        logx = bucket[s, span, :].astype(jnp.float32) * log_step
        resid = weight[span, :] * (score + br + bc - logx)
        res_high, res_low = split(resid)
        four = lax.dot_general(
            jnp.concatenate([res_high, res_low], axis=0), grad_rhs[...],
            (((1,), (1,)), ((), ())), preferred_element_type=jnp.float32)
        rank = rows.shape[1]
        du = (four[:LANES, :rank] + four[:LANES, rank:]) + (four[LANES:, :rank] + four[LANES:, rank:])
        turned_high, turned_low = split(rows.T)
        dv = jnp.dot(
            jnp.concatenate([turned_high, turned_low, turned_high], axis=1),
            jnp.concatenate([res_high, res_high, res_low], axis=0),
            preferred_element_type=jnp.float32)
        parts = lane_parts(resid)
        dbr = jnp.sum(functools.reduce(jnp.add, parts).T, axis=0, keepdims=True)
        dbc = jnp.sum(resid, axis=0, keepdims=True)
        new_br, new_gbr = adagrad(rb[s, k : k + 1, :], rb[s, half + k : half + k + 1, :], dbr)
        rb[s, k : k + 1, :] = new_br
        rb[s, half + k : half + k + 1, :] = new_gbr
        return du, dv, dbc

    def update_cols(s, dv, dbc):
        v[s], gv[s] = adagrad(v[s], gv[s], dv)
        for j, part in enumerate(lane_parts(dbc)):
            new_bc, new_gbc = adagrad(cb[s, j : j + 1, :], cb[s, half + j : half + j + 1, :], part)
            cb[s, j : j + 1, :] = new_bc
            cb[s, half + j : half + j + 1, :] = new_gbc

    def arrived(ref, sem):
        pltpu.make_async_copy(ref, ref, sem).wait()

    @pl.loop(0, strata)
    def _(s):
        @pl.when(s > 0)
        def _():
            for which, ref in ((3, rb), (2, cb), (0, v)):
                arrived(ref.at[s], v_recv.at[s, which])

        split_cols(v[s])
        bc = bias_row(s)
        dv, dbc = 0.0, 0.0
        for k in range(tiles):
            arrived(u.at[s, k], u_recv.at[s, k])
            du, more_dv, more_dbc = tile_grads(s, k, u[s, k], bc)
            grad_u[k] = du
            dv, dbc = dv + more_dv, dbc + more_dbc

        @pl.when(s > 0)
        def _():
            arrived(gv.at[s], v_recv.at[s, 1])

        update_cols(s, dv, dbc)

        @pl.when(s == 0)
        def _():
            pl.semaphore_wait(barrier, partners)

        split_cols(v[s])
        bc = bias_row(s)
        dv, dbc = 0.0, 0.0
        for k in range(tiles):
            arrived(gu.at[s, k], gu_recv.at[s, k])
            rows, accum = adagrad(u[s, k], gu[s, k], grad_u[k])
            du, more_dv, more_dbc = tile_grads(s, k, rows, bc)
            dv, dbc = dv + more_dv, dbc + more_dbc
            u[s, k], gu[s, k] = adagrad(rows, accum, du)

            @pl.when(s < last)
            def _():
                send_u(s, k).start()

            @pl.when(s == last)
            def _():
                home_u(k).start()

        update_cols(s, dv, dbc)

        @pl.when(s < last)
        def _():
            send_v(s, 3).start()
            send_v(s, 2).start()
            send_v(s, 0).start()
            pltpu.make_async_copy(buckets.at[s + 1], bucket.at[s + 1], bucket_sem.at[s + 1]).wait()
            prepare(s + 1)
            send_v(s, 0).wait_send()
            send_v(s, 1).start()
            for k in range(tiles):
                send_u(s, k).wait_send()
                send_gu(s, k).start()

    home_br().start()
    home_bc().start()
    col_out[...] = v[last].T
    home_v().start()

    @pl.loop(0, last)
    def _(s):
        for k in range(tiles):
            send_gu(s, k).wait_send()
        for which in range(1, 4):
            send_v(s, which).wait_send()

    home_br().wait()
    home_bc().wait()
    out_br[...] = bias_home[0, 0:tiles, :]
    out_bc[...] = bias_home[1, 0:tiles, :]
    for k in range(tiles):
        home_u(k).wait()
    home_v().wait()


def shards(
    n_row,
    n_col,
    row_factors,
    row_accum,
    row_bias,
    row_bias_accum,
    col_factors,
    col_accum,
    col_bias,
    col_bias_accum,
    buckets,
    live_pairs,
):
    strata, block, _ = buckets.shape
    rank = row_factors.shape[1]
    tiles = block // LANES
    biases = [b.reshape(tiles, LANES) for b in (row_bias, row_bias_accum, col_bias, col_bias_accum)]
    packed = 2 * (-(-tiles // 4) * 4)
    f32, bf16 = jnp.float32, jnp.bfloat16
    hbm = pl.BlockSpec(memory_space=pltpu.HBM)
    vmem = pl.BlockSpec(memory_space=pltpu.VMEM)
    smem = pl.BlockSpec(memory_space=pltpu.SMEM)
    dma = pltpu.SemaphoreType.DMA
    factors = jax.ShapeDtypeStruct((block, rank), f32)
    bias = jax.ShapeDtypeStruct((tiles, LANES), f32)
    new_u, new_br, new_v, new_bc = pl.pallas_call(
        functools.partial(kernel, n_row, n_col),
        out_shape=(factors, bias, factors, bias),
        in_specs=[hbm] * 9 + [smem],
        out_specs=(hbm, vmem, hbm, vmem),
        scratch_shapes=[
            pltpu.VMEM((strata, tiles, LANES, rank), f32),
            pltpu.VMEM((strata, tiles, LANES, rank), f32),
            pltpu.VMEM((strata, packed, LANES), f32),
            pltpu.VMEM((strata, rank, block), f32),
            pltpu.VMEM((strata, rank, block), f32),
            pltpu.VMEM((strata, packed, LANES), f32),
            pltpu.VMEM((2, block, rank), f32),
            pltpu.VMEM((4, tiles, LANES), f32),
            pltpu.VMEM((block, rank), f32),
            pltpu.VMEM((2, packed, LANES), f32),
            pltpu.VMEM((strata, block, block), jnp.int32),
            pltpu.VMEM((block, block), f32),
            pltpu.VMEM((3 * rank, block), bf16),
            pltpu.VMEM((2 * rank, block), bf16),
            pltpu.VMEM((tiles, LANES, rank), f32),
            dma((strata, tiles)),
            dma((strata, tiles)),
            dma((strata, tiles)),
            dma((strata, tiles)),
            dma((strata + 2, 4)),
            dma((strata, 4)),
            dma((6,)),
            dma((strata,)),
            dma((tiles + 3,)),
        ],
        compiler_params=pltpu.CompilerParams(
            collective_id=0, has_side_effects=True, vmem_limit_bytes=VMEM_BYTES
        ),
    )(
        row_factors, row_accum, biases[0], biases[1],
        col_factors, col_accum, biases[2], biases[3],
        buckets, live_pairs.T,
    )
    new_u, new_br, new_v, new_bc = pl.pallas_call(
        write_out,
        out_shape=(factors, bias, factors, bias),
        in_specs=[hbm] * 4,
        out_specs=(hbm,) * 4,
        scratch_shapes=[
            pltpu.VMEM((block, rank), f32),
            pltpu.VMEM((tiles, LANES), f32),
            pltpu.VMEM((block, rank), f32),
            pltpu.VMEM((tiles, LANES), f32),
            dma((2, 4)),
        ],
        compiler_params=pltpu.CompilerParams(vmem_limit_bytes=VMEM_BYTES),
    )(new_u, new_br, new_v, new_bc)
    return (new_u, new_br.reshape(block), new_v, new_bc.reshape(block))


def solution(mesh):
    in_specs = (
        P(("grp", "row", "col"), None),
        P(("grp", "row", "col"), None),
        P(("grp", "row", "col")),
        P(("grp", "row", "col")),
        P(("grp", "row", "col"), None),
        P(("grp", "row", "col"), None),
        P(("grp", "row", "col")),
        P(("grp", "row", "col")),
        P(None, ("grp", "row", "col"), None),
        P(None, ("grp", "row", "col")),
    )
    out_specs = (
        P(("grp", "row", "col"), None),
        P(("grp", "row", "col")),
        P(("grp", "row", "col"), None),
        P(("grp", "row", "col")),
    )
    body = functools.partial(shards, mesh.shape["row"], mesh.shape["col"])
    return jax.shard_map(body, mesh=mesh, in_specs=in_specs, out_specs=out_specs, check_vma=False)
```
